32 devices in a mesh: wide: 8 (over z, y), narrow: 4 (over x, core).
Axes of the slice: x: 2, y: 2, z: 4, core: 2. Of those that a mesh axis runs over, the one named last changes fastest.
Arguments:
- matrix: float32 [65536, 1024], P(('wide', 'narrow')), may hold values from -0.078125 to 0.078125
- hashes: int32 [65536], P(('wide', 'narrow')), may hold values from 0 to 2047
- sign_bits: int32 [65536], P(('wide', 'narrow')), may hold values from 0 to 1
- targets: float32 [8, 65536], P(None, ('wide', 'narrow')), may hold values from -6 to 6
Outputs:
- r_factor: float32 [1024, 1024], P('narrow')
- projected: float32 [8, 1024], replicated
- estimate: float32 [8, 1024], replicated
The draws below stay inside these ranges and needn't reach their ends.
All inputs are finite; a program needn't handle non-finite values.
Results may differ from the reference program's by a relative error of at most 0.0003.
Values sent between devices are 32-bit elements; how exact they have to be, the bound alone decides.
No kernel may reach another device: no remote copies, remote signals or barrier semaphores. Data moves between devices by JAX's collectives and lax.ppermute only.
A program may use at most 128 MiB of HBM per device.

```python
import jax
import jax.numpy as jnp
from jax import lax

N = 1024
S = 2048
RHS = 8
ROWS = 65536


def draw_matrix(key, part):
    base_key = jax.random.fold_in(key, 11)
    scale_key = jax.random.fold_in(key, 12)
    normal_part = jnp.clip(jax.random.normal(base_key, (ROWS, N), jnp.float32), -6.0, 6.0)
    mixed_cols = normal_part + 0.3 * jnp.roll(normal_part, 1, axis=1) + 0.2 * jnp.roll(normal_part, 5, axis=1)
    scales = jnp.exp(jax.random.uniform(scale_key, (N,), jnp.float32, -0.6931472, 0.6931472))
    return mixed_cols * scales[None, :] / jnp.sqrt(jnp.float32(1.13 * ROWS))


def place_ends(result, own_key, smallest, high):
    extent = result.shape
    index_at = [jax.random.randint(jax.random.fold_in(own_key, axis), (), 0, extent[axis]) for axis in range(len(extent))]
    result = result.at[tuple(index_at)].set(smallest)
    longest = extent.index(max(extent))
    index_at[longest] = (index_at[longest] + 1) % extent[longest]
    return result.at[tuple(index_at)].set(high)


def block_levels(stream_key, shape, split, smallest, top_value):
    gain = 1.0
    for position, parts in split:
        draws = jax.random.uniform(jax.random.fold_in(jax.random.fold_in(stream_key, 6), position), (parts,), jnp.float32, smallest / len(split), top_value / len(split))
        gain = gain * jnp.repeat(jnp.exp(draws), shape[position] // parts).reshape((-1,) + (1,) * (len(shape) - 1 - position))
    return gain


def gaussian(rng, dims, scale, most, split=(), kind=jnp.bfloat16):
    array = scale * jax.random.normal(rng, dims, jnp.float32)
    if split:
        array = array * block_levels(rng, dims, split, -0.22, 0.18)
    return jnp.clip(array, -most, most).astype(kind)


def setup_inputs(seed: int = 0) -> dict:
    key_of = jax.random.split(jax.random.key(seed), 5)
    return {
        "matrix": draw_matrix(jax.random.fold_in(key_of[4], 71), 0),
        "hashes": place_ends(jax.random.randint(key_of[1], (ROWS,), 0, S), jax.random.fold_in(key_of[1], 1), 0, S - 1).astype(jnp.int32),
        "sign_bits": place_ends(jax.random.randint(key_of[2], (ROWS,), 0, 2), jax.random.fold_in(key_of[2], 1), 0, 1).astype(jnp.int32),
        "targets": gaussian(key_of[3], (RHS, ROWS), 1.0, 6.0, ((1, 32),), jnp.float32),
    }


def reference(matrix, hashes, sign_bits, targets):
    row_signs = (2 * sign_bits - 1).astype(jnp.float32)
    sketch = jax.ops.segment_sum(matrix * row_signs[:, None], hashes, num_segments=S)
    upper_factor = jnp.linalg.qr(sketch, mode='r')
    diag_sign = jnp.where(jnp.diagonal(upper_factor) < 0, -1.0, 1.0).astype(jnp.float32)
    r_factor = upper_factor * diag_sign[:, None]
    moments = jnp.dot(targets.astype(jnp.float32), matrix.astype(jnp.float32), precision=lax.Precision.HIGHEST, preferred_element_type=jnp.float32)
    projected = jax.scipy.linalg.solve_triangular(r_factor.T, moments.T, lower=True).T
    estimate = jax.scipy.linalg.solve_triangular(r_factor, projected.T, lower=False).T
    return (r_factor, projected, estimate)
```

```python
import functools

import jax
import jax.numpy as jnp
from jax import lax
from jax.experimental import pallas as pl
from jax.experimental.pallas import tpu as pltpu
from jax.sharding import PartitionSpec as P

S = 2048
NB = 128
F32 = jnp.float32
BF = jnp.bfloat16

def split2(x):
    hi = x.astype(BF)
    lo = (x - hi.astype(F32)).astype(BF)
    return hi, lo

def dg(a, b, dims):
    return lax.dot_general(a, b, (dims, ((), ())), preferred_element_type=F32)

def dot3(a, b, dims=((1,), (0,))):
    ah, al = split2(a)
    bh, bl = split2(b)
    return dg(ah, bl, dims) + dg(al, bh, dims) + dg(ah, bh, dims)

def lane_bcast(x, c):
    return jnp.broadcast_to(x[:, c:c + 1], (8, NB))

def row_bcast(x, i):
    return jnp.broadcast_to(x[i:i + 1, :], (8, NB))

def gather_lanes(x, idx):
    return jnp.take_along_axis(x, idx, axis=1)

def diag_block(D, lane, sub):
    n = NB // 8
    A = list(D)
    T = [jnp.where(lane == sub + 8 * p, 1.0, 0.0).astype(F32) for p in range(n)]
    Rout, Tout = [], []
    for p in range(n):
        Ap, Tp = A[p], T[p]
        S = {}
        for k in range(8):
            bk = lane_bcast(Ap, 8 * p + k)
            for i in range(k, 8):
                S[i, k] = row_bcast(bk, i)
        rows = [row_bcast(Ap, i) for i in range(8)]
        trows = [row_bcast(Tp, i) for i in range(8)]
        for j in range(8):
            r = lax.rsqrt(S[j, j])
            rows[j] = rows[j] * r
            trows[j] = trows[j] * r
            ls = {}
            for i in range(j + 1, 8):
                ls[i] = S[i, j] * r
            for i in range(j + 1, 8):
                for k in range(j + 1, i + 1):
                    S[i, k] = S[i, k] - ls[i] * ls[k]
                rows[i] = rows[i] - ls[i] * rows[j]
                trows[i] = trows[i] - ls[i] * trows[j]
        Rp, Tpp = rows[0], trows[0]
        for j in range(1, 8):
            Rp = jnp.where(sub == j, rows[j], Rp)
            Tpp = jnp.where(sub == j, trows[j], Tpp)
        Rout.append(jnp.where(lane >= sub + 8 * p, Rp, 0.0))
        Tout.append(jnp.where(lane <= sub + 8 * p, Tpp, 0.0))
        for q in range(p + 1, n):
            idx = sub + 8 * q
            for j in range(8):
                c = gather_lanes(rows[j], idx)
                A[q] = A[q] - c * rows[j]
                T[q] = T[q] - c * trows[j]
    return Rout, Tout

def chol_kernel(nblk, share, idx_ref, g_ref, m_ref, r_out, y_out, x_out, a, t, m):
    W = nblk * NB
    lane = lax.broadcasted_iota(jnp.int32, (8, NB), 1)
    sub = lax.broadcasted_iota(jnp.int32, (8, NB), 0)
    a[...] = g_ref[...]
    m[...] = m_ref[...]

    def step(k, carry):
        o = pl.multiple_of(k * NB, NB)
        D = [a[pl.ds(pl.multiple_of(o + 8 * p, 8), 8), pl.ds(o, NB)] for p in range(NB // 8)]
        R, T = diag_block(D, lane, sub)
        for p in range(NB // 8):
            a[pl.ds(pl.multiple_of(o + 8 * p, 8), 8), pl.ds(o, NB)] = R[p]
            t[pl.ds(pl.multiple_of(o + 8 * p, 8), 8), :] = T[p]
        Tm = t[pl.ds(o, NB), :]
        yk = dot3(m[:, pl.ds(o, NB)], Tm, ((1,), (1,)))
        m[:, pl.ds(o, NB)] = yk
        for j in range(nblk):
            js = slice(j * NB, (j + 1) * NB)
            @pl.when(j < k)
            def _():
                a[pl.ds(o, NB), js] = jnp.zeros((NB, NB), F32)
            @pl.when(j > k)
            def _():
                rj = dot3(Tm, a[pl.ds(o, NB), js])
                a[pl.ds(o, NB), js] = rj
                m[:, js] = m[:, js] - dot3(yk, rj)
        for i in range(1, nblk):
            @pl.when(i > k)
            def _():
                is_ = slice(i * NB, (i + 1) * NB)
                rest = slice(i * NB, W)
                lhs = a[pl.ds(o, NB), is_]
                a[is_, rest] = a[is_, rest] - dot3(lhs, a[pl.ds(o, NB), rest], ((0,), (0,)))
        return carry
    lax.fori_loop(0, nblk, step, 0)
    y_out[...] = m[...]
    for k in range(nblk - 1, -1, -1):
        ks = slice(k * NB, (k + 1) * NB)
        xk = dot3(m[:, ks], t[ks, :])
        x_out[:, ks] = xk
        if k:
            m[:, :k * NB] = m[:, :k * NB] - dot3(xk, a[:k * NB, ks], ((1,), (1,)))
    r_out[...] = a[pl.ds(pl.multiple_of(idx_ref[0] * share, share), share), :]

def cholesky(gram, moments, index, share):
    W = gram.shape[0]
    nblk = W // NB
    vm = pl.BlockSpec(memory_space=pltpu.VMEM)
    return pl.pallas_call(
        functools.partial(chol_kernel, nblk, share),
        out_shape=(jax.ShapeDtypeStruct((share, W), F32),
                   jax.ShapeDtypeStruct(moments.shape, F32),
                   jax.ShapeDtypeStruct(moments.shape, F32)),
        in_specs=[pl.BlockSpec(memory_space=pltpu.SMEM), vm, vm],
        out_specs=(vm, vm, vm),
        scratch_shapes=[pltpu.VMEM((W, W), F32), pltpu.VMEM((W, NB), F32), pltpu.VMEM(moments.shape, F32)],
        compiler_params=pltpu.CompilerParams(vmem_limit_bytes=40 * 2**20),
        name="factor",
    )(index, gram, moments)


def shards(matrix, hashes, sign_bits, targets):
    rows_local = matrix.shape[0]
    width = matrix.shape[1]
    row_signs = (2 * sign_bits - 1).astype(jnp.float32)
    block = min(512, rows_local)
    block_count = rows_local // block
    bucket_range = lax.iota(jnp.int32, S)

    def add_block(block_index, running):
        offset = block_index * block
        bucket_ids = lax.dynamic_slice_in_dim(hashes, offset, block, 0)
        block_signs = lax.dynamic_slice_in_dim(row_signs, offset, block, 0)
        block_rows = lax.dynamic_slice_in_dim(matrix, offset, block, 0)
        one_hot = jnp.where(bucket_range[:, None] == bucket_ids[None, :], block_signs[None, :], 0.0)
        return running + jnp.dot(
            one_hot, block_rows, precision=lax.Precision.HIGHEST, preferred_element_type=jnp.float32
        )

    partial_sketch = lax.fori_loop(0, block_count, add_block, jnp.zeros((S, width), jnp.float32))
    moments_local = jnp.dot(
        targets, matrix, precision=lax.Precision.HIGHEST, preferred_element_type=jnp.float32
    )
    owned_rows = lax.psum_scatter(
        partial_sketch, ("wide", "narrow"), scatter_dimension=0, tiled=True
    )
    gram_matrix, moments = lax.psum(
        (
            lax.dot_general(
                owned_rows,
                owned_rows,
                (((0,), (0,)), ((), ())),
                precision=lax.Precision.HIGHEST,
                preferred_element_type=jnp.float32,
            ),
            moments_local,
        ),
        ("wide", "narrow"),
    )
    share = width // lax.axis_size("narrow")
    index = lax.axis_index("narrow").astype(jnp.int32).reshape(1)
    return cholesky(gram_matrix, moments, index, share)


def solution(mesh):
    return jax.shard_map(
        shards,
        mesh=mesh,
        in_specs=(
            P(("wide", "narrow"), None),
            P(("wide", "narrow")),
            P(("wide", "narrow")),
            P(None, ("wide", "narrow")),
        ),
        out_specs=(P("narrow", None), P(), P()),
        check_vma=False,
    )
```

```python
import functools

import jax
import jax.numpy as jnp
from jax import lax
from jax.experimental import pallas as pl
from jax.experimental.pallas import tpu as pltpu
from jax.sharding import PartitionSpec as P

S = 2048
NB = 128
F32 = jnp.float32
BF = jnp.bfloat16


def split2(x):
    hi = x.astype(BF)
    lo = (x - hi.astype(F32)).astype(BF)
    return hi, lo


def dg(a, b, dims):
    return lax.dot_general(a, b, (dims, ((), ())), preferred_element_type=F32)


def dot3(a, b, dims=((1,), (0,))):
    ah, al = split2(a)
    bh, bl = split2(b)
    return dg(ah, bl, dims) + dg(al, bh, dims) + dg(ah, bh, dims)


def lane_bcast(x, c):
    return jnp.broadcast_to(x[:, c:c + 1], (8, NB))


def row_bcast(x, i):
    return jnp.broadcast_to(x[i:i + 1, :], (8, NB))


def gather_lanes(x, idx):
    return jnp.take_along_axis(x, idx, axis=1)


def diag_block(D, lane, sub):
    n = NB // 8
    A = list(D)
    T = [jnp.where(lane == sub + 8 * p, 1.0, 0.0).astype(F32) for p in range(n)]
    Rout, Tout = [], []
    for p in range(n):
        Ap, Tp = A[p], T[p]
        C = {}
        for k in range(8):
            bk = lane_bcast(Ap, 8 * p + k)
            for i in range(k, 8):
                C[i, k] = row_bcast(bk, i)
        rows = [row_bcast(Ap, i) for i in range(8)]
        trows = [row_bcast(Tp, i) for i in range(8)]
        for j in range(8):
            r = lax.rsqrt(C[j, j])
            rows[j] = rows[j] * r
            trows[j] = trows[j] * r
            ls = {}
            for i in range(j + 1, 8):
                ls[i] = C[i, j] * r
            for i in range(j + 1, 8):
                for k in range(j + 1, i + 1):
                    C[i, k] = C[i, k] - ls[i] * ls[k]
                rows[i] = rows[i] - ls[i] * rows[j]
                trows[i] = trows[i] - ls[i] * trows[j]
        Rp, Tpp = rows[0], trows[0]
        for j in range(1, 8):
            Rp = jnp.where(sub == j, rows[j], Rp)
            Tpp = jnp.where(sub == j, trows[j], Tpp)
        Rout.append(jnp.where(lane >= sub + 8 * p, Rp, 0.0))
        Tout.append(jnp.where(lane <= sub + 8 * p, Tpp, 0.0))
        for q in range(p + 1, n):
            idx = sub + 8 * q
            for j in range(8):
                c = gather_lanes(rows[j], idx)
                A[q] = A[q] - c * rows[j]
                T[q] = T[q] - c * trows[j]
    return Rout, Tout


def panel_kernel(J, share, heights, half, *refs):
    n = len(heights)
    idx_ref, refs = refs[0], refs[1:]
    g_refs, refs = refs[:n], refs[n:]
    w_refs, refs = refs[:J], refs[J:]
    m_ref, x_ref, r_out, w_out, y_out, x_out, col, rcol = refs
    lane = lax.broadcasted_iota(jnp.int32, (8, NB), 1)
    sub = lax.broadcasted_iota(jnp.int32, (8, NB), 0)
    at = 0
    for ref, height in zip(g_refs, heights):
        col[at:at + height, :] = ref[:height, half * NB:(half + 1) * NB]
        at += height
    rcol[...] = jnp.zeros(rcol.shape, F32)
    o = J * NB
    D = col[o:o + NB, :]
    if J:
        gh, gl = split2(col[:o, :])
        V = [None] * J
        for i in range(J):
            e = (i + 1) * NB
            wh, wl = split2(w_refs[i][...])
            nn = ((1,), (0,))
            ri = dg(wh, gl[:e], nn) + dg(wl, gh[:e], nn) + dg(wh, gh[:e], nn)
            rcol[i * NB:e, :] = ri
            rt = ri.T
            D = D - dot3(rt, ri)
            th, tl = split2(rt)
            v = dg(th, wl, nn) + dg(tl, wh, nn) + dg(th, wh, nn)
            for l in range(i + 1):
                piece = v[:, l * NB:(l + 1) * NB]
                V[l] = piece if V[l] is None else V[l] + piece
    col[o:o + NB, :] = D
    R, T = diag_block([col[o + 8 * p:o + 8 * p + 8, :] for p in range(NB // 8)], lane, sub)
    for p in range(NB // 8):
        rcol[o + 8 * p:o + 8 * p + 8, :] = R[p]
        w_out[8 * p:8 * p + 8, o:o + NB] = T[p]
    if J:
        w_out[:, :o] = -dot3(w_out[:, o:o + NB], jnp.concatenate(V, axis=1))
    W = w_out[...]
    y = dot3(m_ref[:, :o + NB], W, ((1,), (1,)))
    y_out[...] = y
    x_out[...] = x_ref[...]
    x_out[:, :o + NB] = x_ref[:, :o + NB] + dot3(y, W)
    r_out[...] = rcol[pl.ds(pl.multiple_of(idx_ref[0] * share, share), share), :]


def panel(J, share, grams, half, rows, moments, x, index):
    width = moments.shape[1]
    k = moments.shape[0]
    heights = []
    left = (J + 1) * NB
    for g in grams:
        heights.append(min(g.shape[0], left))
        left -= heights[-1]
    vm = pl.BlockSpec(memory_space=pltpu.VMEM)
    shape = lambda *s: jax.ShapeDtypeStruct(s, F32)
    flops = 6 * NB * NB * NB * (2 * J * J + 4)
    return pl.pallas_call(
        functools.partial(panel_kernel, J, share, tuple(heights), half),
        out_shape=(shape(share, NB), shape(NB, (J + 1) * NB), shape(k, NB), shape(k, width)),
        in_specs=[pl.BlockSpec(memory_space=pltpu.SMEM)]
        + [vm] * (len(heights) + J + 2),
        out_specs=(vm,) * 4,
        scratch_shapes=[pltpu.VMEM(((J + 1) * NB, NB), F32), pltpu.VMEM((width, NB), F32)],
        compiler_params=pltpu.CompilerParams(vmem_limit_bytes=40 * 2**20),
        name="panel%d" % J,
    )(index, *grams, *rows, moments, x)


def factor(grams, widths, moments, index, share):
    x = jnp.zeros_like(moments)
    rows, shares, ys = [], [], []
    J = 0
    for c, w in enumerate(widths):
        for half in range(w // NB):
            r, wr, y, x = panel(J, share, grams[c], half, rows, moments, x, index)
            rows.append(wr)
            shares.append(r)
            ys.append(y)
            J += 1
    return jnp.concatenate(shares, axis=1), jnp.concatenate(ys, axis=1), x


WIDTHS = (256, 256, 256, 256)


def exchange_orders(narrow, wide):
    first = [("narrow", 1 << b) for b in range(narrow.bit_length() - 1)]
    first += [("wide", 1 << b) for b in range(wide.bit_length() - 1)]
    second = list(first)
    if len(second) > 2:
        second[1], second[2] = second[2], second[1]
    return first, second


def swap(value, axis, bit):
    size = lax.axis_size(axis)
    return lax.ppermute(value, axis, [(i, i ^ bit) for i in range(size)])


def has_bit(axis, bit):
    return (lax.axis_index(axis) & bit) != 0


def together(*values):
    return lax.optimization_barrier(values)


def reduce_step(values, step):
    half = values.shape[0] // 2
    return values[:half] + swap(values[half:], *step)


def gather_step(values, step):
    other = swap(values, *step)
    upper = has_bit(*step)
    return jnp.concatenate([jnp.where(upper, other, values), jnp.where(upper, values, other)], axis=0)


def halves(x):
    high = lax.reduce_precision(x, 8, 7)
    return high.astype(BF), (x - high).astype(BF)


def gram_block(left, right):
    return lax.dot_general(
        left, right, (((0,), (0,)), ((), ())), precision=lax.Precision.HIGH, preferred_element_type=F32
    )


def shards(matrix, hashes, sign_bits, targets):
    width = matrix.shape[1]
    orders = exchange_orders(lax.axis_size("narrow"), lax.axis_size("wide"))
    steps = len(orders[0]) - 1
    signs = (2 * sign_bits - 1).astype(BF)
    places = lax.iota(jnp.int32, S)
    one_hots = []
    for order in orders:
        mask = jnp.int32(0)
        for step, (axis, bit) in enumerate(order[:-1]):
            mask = mask + jnp.where(has_bit(axis, bit), S >> (step + 1), 0)
        one_hots.append(jnp.where(places[:, None] == (hashes ^ mask)[None, :], signs[None, :], 0).astype(BF))

    def sketch(c, columns):
        high, low = halves(columns)
        one_hot = one_hots[c % 2]
        return jnp.dot(one_hot, high, preferred_element_type=F32) + jnp.dot(one_hot, low, preferred_element_type=F32)

    def down(c, t):
        part[c] = reduce_step(part[c], orders[c % 2][t])

    def across(c):
        part[c] = part[c] + swap(part[c], *orders[0][-1])

    def up(c, t):
        part[c] = gather_step(part[c], orders[c % 2][t])

    def line(c, lowest):
        for t in range(3, steps):
            down(c, t)
        across(c)
        for t in range(steps - 1, lowest - 1, -1):
            up(c, t)

    bounds = [sum(WIDTHS[:c]) for c in range(len(WIDTHS) + 1)]
    cols = [matrix[:, bounds[c]:bounds[c + 1]] for c in range(4)]
    part = [sketch(0, cols[0]), None, None, None]
    part[0], cols[1] = together(part[0], cols[1])
    down(0, 0)
    part[1] = sketch(1, cols[1])
    part[0], part[1], cols[2], cols[3] = together(part[0], part[1], cols[2], cols[3])
    down(1, 0)
    part[2] = sketch(2, cols[2])
    part[0], part[1], part[2], cols[3] = together(part[0], part[1], part[2], cols[3])
    down(0, 1)
    down(1, 1)
    down(2, 0)
    part[3] = sketch(3, cols[3])
    part[0], part[1], part[2], part[3], matrix = together(*part, matrix)
    down(0, 2)
    down(1, 2)
    down(3, 0)
    moments = jnp.dot(targets, matrix, precision=lax.Precision.HIGH, preferred_element_type=F32)
    *part, moments = together(*part, moments)
    down(2, 1)
    down(3, 1)
    line(0, 4)
    line(1, 4)
    moments = moments + swap(moments, *orders[0][0])
    *part, moments = together(*part, moments)
    down(2, 2)
    down(3, 2)
    for c in range(2):
        for t in range(min(3, steps - 1), 2, -1):
            up(c, t)
    moments = moments + swap(moments, *orders[0][1])
    *part, moments = together(*part, moments)
    up(0, 2)
    up(1, 2)
    line(2, 3)
    line(3, 3)
    moments = moments + swap(moments, *orders[0][2])
    *part, moments = together(*part, moments)
    up(0, 1)
    up(1, 1)
    for step in orders[0][3:]:
        moments = moments + swap(moments, *step)
    *part, moments = together(*part, moments)
    up(0, 0)
    up(1, 0)
    up(2, 2)
    up(3, 2)
    *part, moments = together(*part, moments)
    share = width // lax.axis_size("narrow")
    index = lax.axis_index("narrow").astype(jnp.int32).reshape(1)
    x = jnp.zeros_like(moments)
    rows, shares, ys = [], [], []

    def panels(grams, half, x):
        r, wr, y, x = panel(len(rows), share, grams, half, rows, moments, x, index)
        rows.append(wr)
        shares.append(r)
        ys.append(y)
        return x

    left = jnp.concatenate(part[:2], axis=1)
    up(2, 1)
    up(3, 1)
    column = [gram_block(left, left)]
    x = panels(column, 0, x)
    x = panels(column, 1, x)
    *part, x = together(*part, x)
    up(2, 0)
    up(3, 0)
    x = panels(column, 2, x)
    *part, x = together(*part, x)
    right = jnp.concatenate(part[2:], axis=1)
    x = panels(column, 3, x)
    column = [gram_block(left, right), gram_block(right, right)]
    for half in range(4):
        x = panels(column, half, x)
    return jnp.concatenate(shares, axis=1), jnp.concatenate(ys, axis=1), x


def solution(mesh):
    return jax.shard_map(
        shards,
        mesh=mesh,
        in_specs=(
            P(("wide", "narrow"), None),
            P(("wide", "narrow")),
            P(("wide", "narrow")),
            P(None, ("wide", "narrow")),
        ),
        out_specs=(P("narrow", None), P(), P()),
        check_vma=False,
    )
```

```python
import functools

import jax
import jax.numpy as jnp
from jax import lax
from jax.experimental import pallas as pl
from jax.experimental.pallas import tpu as pltpu
from jax.sharding import PartitionSpec as P

S = 2048
NB = 128
F32 = jnp.float32
BF = jnp.bfloat16


def split2(x):
    hi = x.astype(BF)
    lo = (x - hi.astype(F32)).astype(BF)
    return hi, lo


def dg(a, b, dims):
    return lax.dot_general(a, b, (dims, ((), ())), preferred_element_type=F32)


def dot3(a, b, dims=((1,), (0,))):
    ah, al = split2(a)
    bh, bl = split2(b)
    return dg(ah, bl, dims) + dg(al, bh, dims) + dg(ah, bh, dims)


def lane_bcast(x, c):
    return jnp.broadcast_to(x[:, c:c + 1], (8, NB))


def row_bcast(x, i):
    return jnp.broadcast_to(x[i:i + 1, :], (8, NB))


def gather_lanes(x, idx):
    return jnp.take_along_axis(x, idx, axis=1)


def diag_block(D, lane, sub):
    n = NB // 8
    A = list(D)
    T = [jnp.where(lane == sub + 8 * p, 1.0, 0.0).astype(F32) for p in range(n)]
    Rout, Tout = [], []
    for p in range(n):
        Ap, Tp = A[p], T[p]
        C = {}
        for k in range(8):
            bk = lane_bcast(Ap, 8 * p + k)
            for i in range(k, 8):
                C[i, k] = row_bcast(bk, i)
        rows = [row_bcast(Ap, i) for i in range(8)]
        trows = [row_bcast(Tp, i) for i in range(8)]
        for j in range(8):
            r = lax.rsqrt(C[j, j])
            rows[j] = rows[j] * r
            trows[j] = trows[j] * r
            ls = {}
            for i in range(j + 1, 8):
                ls[i] = C[i, j] * r
            for i in range(j + 1, 8):
                for k in range(j + 1, i + 1):
                    C[i, k] = C[i, k] - ls[i] * ls[k]
                rows[i] = rows[i] - ls[i] * rows[j]
                trows[i] = trows[i] - ls[i] * trows[j]
        Rp, Tpp = rows[0], trows[0]
        for j in range(1, 8):
            Rp = jnp.where(sub == j, rows[j], Rp)
            Tpp = jnp.where(sub == j, trows[j], Tpp)
        Rout.append(jnp.where(lane >= sub + 8 * p, Rp, 0.0))
        Tout.append(jnp.where(lane <= sub + 8 * p, Tpp, 0.0))
        for q in range(p + 1, n):
            idx = sub + 8 * q
            for j in range(8):
                c = gather_lanes(rows[j], idx)
                A[q] = A[q] - c * rows[j]
                T[q] = T[q] - c * trows[j]
    return Rout, Tout


def panel_kernel(J, n, share, parts, priors, *refs):
    nn, nt = ((1,), (0,)), ((1,), (1,))
    idx_ref, refs = refs[0], refs[1:]
    g_refs, refs = refs[:len(parts)], refs[len(parts):]
    w_refs, refs = refs[:len(priors)], refs[len(priors):]
    m_ref, x_ref, r_out, w_out, y_out, x_out, rcol, d, v = refs
    lane = lax.broadcasted_iota(jnp.int32, (8, NB), 1)
    sub = lax.broadcasted_iota(jnp.int32, (8, NB), 0)
    o, w = J * NB, n * NB
    at, above = 0, []
    for ref, (height, left) in zip(g_refs, parts):
        take = min(height, max(o - at, 0))
        if take:
            above.append(ref[:take, left:left + w])
        if take < height:
            first = at + take - o
            d[first:first + height - take, :] = ref[take:height, left:left + w]
        at += height
    rcol[...] = jnp.zeros(rcol.shape, F32)
    w_out[...] = jnp.zeros(w_out.shape, F32)
    v[...] = jnp.zeros(v.shape, F32)
    if J:
        gh, gl = split2(jnp.concatenate(above, axis=0) if len(above) > 1 else above[0])
        for ref, (first, blocks) in zip(w_refs, priors):
            f, e = first * NB, (first + blocks) * NB
            wh, wl = split2(ref[...])
            ri = dg(wh, gl[:e], nn) + dg(wl, gh[:e], nn) + dg(wh, gh[:e], nn)
            rcol[f:e, :] = ri
            rh, rl = split2(ri)
            th, tl = split2(ri.T)
            for q in range(n):
                rows = slice(q * NB, (q + 1) * NB)
                cut = slice(q * NB, w)
                d[rows, cut] = d[rows, cut] - (
                    dg(th[rows], rl[:, cut], nn) + dg(tl[rows], rh[:, cut], nn) + dg(th[rows], rh[:, cut], nn))
            v[:, :e] = v[:, :e] + (dg(th, wl, nn) + dg(tl, wh, nn) + dg(th, wh, nn))
    for p in range(n):
        rows = slice(p * NB, (p + 1) * NB)
        e = o + (p + 1) * NB
        R, T = diag_block([d[p * NB + 8 * i:p * NB + 8 * i + 8, rows] for i in range(NB // 8)], lane, sub)
        for i in range(NB // 8):
            rcol[o + p * NB + 8 * i:o + p * NB + 8 * i + 8, rows] = R[i]
            w_out[p * NB + 8 * i:p * NB + 8 * i + 8, e - NB:e] = T[i]
        Tm = w_out[rows, e - NB:e]
        if p + 1 < n:
            rest = slice((p + 1) * NB, w)
            rq = dot3(Tm, d[rows, rest])
            rcol[o + p * NB:o + (p + 1) * NB, rest] = rq
            rt = rq.T
            d[rest, rest] = d[rest, rest] - dot3(rt, rq)
        if e > NB:
            w_out[rows, :e - NB] = -dot3(Tm, v[rows, :e - NB])
        if p + 1 < n:
            v[rest, :e] = v[rest, :e] + dot3(rt, w_out[rows, :e])
    W = w_out[...]
    y = dot3(m_ref[:, :o + w], W, nt)
    y_out[...] = y
    x_out[...] = x_ref[...]
    x_out[:, :o + w] = x_ref[:, :o + w] + dot3(y, W)
    r_out[...] = rcol[pl.ds(pl.multiple_of(idx_ref[0] * share, share), share), :]


def panel(J, n, share, grams, left, priors, moments, x, index):
    width = moments.shape[1]
    k = moments.shape[0]
    parts, rest = [], (J + n) * NB
    for g in grams:
        parts.append((min(g.shape[0], rest), left))
        rest -= parts[-1][0]
    vm = pl.BlockSpec(memory_space=pltpu.VMEM)
    shape = lambda *s: jax.ShapeDtypeStruct(s, F32)
    return pl.pallas_call(
        functools.partial(panel_kernel, J, n, share, tuple(parts), tuple(q[:2] for q in priors)),
        out_shape=(shape(share, n * NB), shape(n * NB, (J + n) * NB), shape(k, n * NB), shape(k, width)),
        in_specs=[pl.BlockSpec(memory_space=pltpu.SMEM)] + [vm] * (len(grams) + len(priors) + 2),
        out_specs=(vm,) * 4,
        scratch_shapes=[
            pltpu.VMEM((width, n * NB), F32),
            pltpu.VMEM((n * NB, n * NB), F32),
            pltpu.VMEM((n * NB, (J + n) * NB), F32),
        ],
        compiler_params=pltpu.CompilerParams(vmem_limit_bytes=40 * 2**20),
        name="panels%d" % J,
    )(index, *grams, *[q[2] for q in priors], moments, x)


WIDTHS = (256, 256, 256, 256)


def exchange_orders(narrow, wide):
    first = [("narrow", 1 << b) for b in range(narrow.bit_length() - 1)]
    first += [("wide", 1 << b) for b in range(wide.bit_length() - 1)]
    second = list(first)
    if len(second) > 2:
        second[1], second[2] = second[2], second[1]
    return first, second


def swap(value, axis, bit):
    size = lax.axis_size(axis)
    return lax.ppermute(value, axis, [(i, i ^ bit) for i in range(size)])


def has_bit(axis, bit):
    return (lax.axis_index(axis) & bit) != 0


def together(*values):
    return lax.optimization_barrier(values)


def reduce_step(values, step):
    half = values.shape[0] // 2
    return values[:half] + swap(values[half:], *step)


def gather_step(values, step):
    other = swap(values, *step)
    upper = has_bit(*step)
    return jnp.concatenate([jnp.where(upper, other, values), jnp.where(upper, values, other)], axis=0)


def halves(x):
    high = lax.reduce_precision(x, 8, 7)
    return high.astype(BF), (x - high).astype(BF)


def gram_block(left, right):
    return lax.dot_general(
        left, right, (((0,), (0,)), ((), ())), precision=lax.Precision.HIGH, preferred_element_type=F32
    )


def shards(matrix, hashes, sign_bits, targets):
    width = matrix.shape[1]
    orders = exchange_orders(lax.axis_size("narrow"), lax.axis_size("wide"))
    steps = len(orders[0]) - 1
    signs = (2 * sign_bits - 1).astype(BF)
    places = lax.iota(jnp.int32, S)
    one_hots = []
    for order in orders:
        mask = jnp.int32(0)
        for step, (axis, bit) in enumerate(order[:-1]):
            mask = mask + jnp.where(has_bit(axis, bit), S >> (step + 1), 0)
        one_hots.append(jnp.where(places[:, None] == (hashes ^ mask)[None, :], signs[None, :], 0).astype(BF))

    def sketch(c, columns):
        high, low = halves(columns)
        one_hot = one_hots[c % 2]
        return jnp.dot(one_hot, high, preferred_element_type=F32) + jnp.dot(one_hot, low, preferred_element_type=F32)

    def down(c, t):
        part[c] = reduce_step(part[c], orders[c % 2][t])

    def across(c):
        part[c] = part[c] + swap(part[c], *orders[0][-1])

    def up(c, t):
        part[c] = gather_step(part[c], orders[c % 2][t])

    def line(c, lowest):
        for t in range(3, steps):
            down(c, t)
        across(c)
        for t in range(steps - 1, lowest - 1, -1):
            up(c, t)

    bounds = [sum(WIDTHS[:c]) for c in range(len(WIDTHS) + 1)]
    cols = [matrix[:, bounds[c]:bounds[c + 1]] for c in range(4)]
    part = [sketch(0, cols[0]), None, None, None]
    part[0], cols[1] = together(part[0], cols[1])
    down(0, 0)
    part[1] = sketch(1, cols[1])
    part[0], part[1], cols[2], cols[3] = together(part[0], part[1], cols[2], cols[3])
    down(1, 0)
    part[2] = sketch(2, cols[2])
    part[0], part[1], part[2], cols[3] = together(part[0], part[1], part[2], cols[3])
    down(0, 1)
    down(1, 1)
    down(2, 0)
    part[3] = sketch(3, cols[3])
    part[0], part[1], part[2], part[3], matrix = together(*part, matrix)
    down(0, 2)
    down(1, 2)
    down(3, 0)
    moments = jnp.dot(targets, matrix, precision=lax.Precision.HIGH, preferred_element_type=F32)
    *part, moments = together(*part, moments)
    down(2, 1)
    down(3, 1)
    line(0, 4)
    line(1, 4)
    moments = moments + swap(moments, *orders[0][0])
    *part, moments = together(*part, moments)
    down(2, 2)
    down(3, 2)
    for c in range(2):
        for t in range(min(3, steps - 1), 2, -1):
            up(c, t)
    moments = moments + swap(moments, *orders[0][1])
    *part, moments = together(*part, moments)
    up(0, 2)
    up(1, 2)
    line(2, 3)
    line(3, 3)
    moments = moments + swap(moments, *orders[0][2])
    *part, moments = together(*part, moments)
    up(0, 1)
    up(1, 1)
    for step in orders[0][3:]:
        moments = moments + swap(moments, *step)
    *part, moments = together(*part, moments)
    up(0, 0)
    up(1, 0)
    up(2, 2)
    up(3, 2)
    *part, moments = together(*part, moments)
    share = width // lax.axis_size("narrow")
    index = lax.axis_index("narrow").astype(jnp.int32).reshape(1)
    x = jnp.zeros_like(moments)
    priors, shares, ys = [], [], []

    def panels(n, grams, left, x):
        first = sum(q[1] for q in priors)
        r, wr, y, x = panel(first, n, share, grams, left, priors, moments, x, index)
        priors.append((first, n, wr))
        shares.append(r)
        ys.append(y)
        return x

    left = jnp.concatenate(part[:2], axis=1)
    up(2, 1)
    up(3, 1)
    column = [gram_block(left, left)]
    x = panels(2, column, 0, x)
    x = panels(1, column, 2 * NB, x)
    part[2], part[3], x = together(part[2], part[3], x)
    up(2, 0)
    up(3, 0)
    x = panels(1, column, 3 * NB, x)
    part[2], part[3], x = together(part[2], part[3], x)
    right = jnp.concatenate(part[2:], axis=1)
    column = [gram_block(left, right), gram_block(right, right)]
    x = panels(4, column, 0, x)
    return jnp.concatenate(shares, axis=1), jnp.concatenate(ys, axis=1), x


def solution(mesh):
    return jax.shard_map(
        shards,
        mesh=mesh,
        in_specs=(
            P(("wide", "narrow"), None),
            P(("wide", "narrow")),
            P(("wide", "narrow")),
            P(None, ("wide", "narrow")),
        ),
        out_specs=(P("narrow", None), P(), P()),
        check_vma=False,
    )
```

```python
import functools

import jax
import jax.numpy as jnp
from jax import lax
from jax.experimental import pallas as pl
from jax.experimental.pallas import tpu as pltpu
from jax.sharding import PartitionSpec as P

S = 2048
NB = 128
F32 = jnp.float32
BF = jnp.bfloat16


def split2(x):
    hi = x.astype(BF)
    lo = (x - hi.astype(F32)).astype(BF)
    return hi, lo


def dg(a, b, dims):
    return lax.dot_general(a, b, (dims, ((), ())), preferred_element_type=F32)


def dot3(a, b, dims=((1,), (0,))):
    ah, al = split2(a)
    bh, bl = split2(b)
    return dg(ah, bl, dims) + dg(al, bh, dims) + dg(ah, bh, dims)


def lane_bcast(x, c):
    return jnp.broadcast_to(x[:, c:c + 1], (8, NB))


def row_bcast(x, i):
    return jnp.broadcast_to(x[i:i + 1, :], (8, NB))


def gather_lanes(x, idx):
    return jnp.take_along_axis(x, idx, axis=1)


def diag_block(D, lane, sub):
    n = NB // 8
    A = list(D)
    T = [jnp.where(lane == sub + 8 * p, 1.0, 0.0).astype(F32) for p in range(n)]
    Rout, Tout = [], []
    for p in range(n):
        Ap, Tp = A[p], T[p]
        C = {}
        for k in range(8):
            bk = lane_bcast(Ap, 8 * p + k)
            for i in range(k, 8):
                C[i, k] = row_bcast(bk, i)
        rows = [row_bcast(Ap, i) for i in range(8)]
        trows = [row_bcast(Tp, i) for i in range(8)]
        for j in range(8):
            r = lax.rsqrt(C[j, j])
            rows[j] = rows[j] * r
            trows[j] = trows[j] * r
            ls = {}
            for i in range(j + 1, 8):
                ls[i] = C[i, j] * r
            for i in range(j + 1, 8):
                for k in range(j + 1, i + 1):
                    C[i, k] = C[i, k] - ls[i] * ls[k]
                rows[i] = rows[i] - ls[i] * rows[j]
                trows[i] = trows[i] - ls[i] * trows[j]
        Rp, Tpp = rows[0], trows[0]
        for j in range(1, 8):
            Rp = jnp.where(sub == j, rows[j], Rp)
            Tpp = jnp.where(sub == j, trows[j], Tpp)
        Rout.append(jnp.where(lane >= sub + 8 * p, Rp, 0.0))
        Tout.append(jnp.where(lane <= sub + 8 * p, Tpp, 0.0))
        for q in range(p + 1, n):
            idx = sub + 8 * q
            for j in range(8):
                c = gather_lanes(rows[j], idx)
                A[q] = A[q] - c * rows[j]
                T[q] = T[q] - c * trows[j]
    return Rout, Tout


def panel_kernel(J, n, share, parts, priors, done, *refs):
    nn, nt = ((1,), (0,)), ((1,), (1,))
    idx_ref, refs = refs[0], refs[1:]
    g_refs, refs = refs[:len(parts)], refs[len(parts):]
    w_refs, refs = refs[:len(priors)], refs[len(priors):]
    r_refs, y_refs, refs = refs[:done], refs[done:2 * done], refs[2 * done:]
    m_ref, x_ref, r_out, w_out, y_out, x_out, rcol, d, v = refs
    lane = lax.broadcasted_iota(jnp.int32, (8, NB), 1)
    sub = lax.broadcasted_iota(jnp.int32, (8, NB), 0)
    o, w = J * NB, n * NB
    at, above = 0, []
    for ref, (height, left) in zip(g_refs, parts):
        take = min(height, max(o - at, 0))
        if take:
            above.append(ref[:take, left:left + w])
        if take < height:
            first = at + take - o
            d[first:first + height - take, :] = ref[take:height, left:left + w]
        at += height
    rcol[...] = jnp.zeros(rcol.shape, F32)
    w_out[...] = jnp.zeros(w_out.shape, F32)
    v[...] = jnp.zeros(v.shape, F32)
    if J:
        gh, gl = split2(jnp.concatenate(above, axis=0) if len(above) > 1 else above[0])
        for ref, (first, blocks) in zip(w_refs, priors):
            f, e = first * NB, (first + blocks) * NB
            wh, wl = split2(ref[...])
            ri = dg(wh, gl[:e], nn) + dg(wl, gh[:e], nn) + dg(wh, gh[:e], nn)
            rcol[f:e, :] = ri
            rh, rl = split2(ri)
            th, tl = split2(ri.T)
            for q in range(n):
                rows = slice(q * NB, (q + 1) * NB)
                cut = slice(q * NB, w)
                d[rows, cut] = d[rows, cut] - (
                    dg(th[rows], rl[:, cut], nn) + dg(tl[rows], rh[:, cut], nn) + dg(th[rows], rh[:, cut], nn))
            v[:, :e] = v[:, :e] + (dg(th, wl, nn) + dg(tl, wh, nn) + dg(th, wh, nn))
    for p in range(n):
        rows = slice(p * NB, (p + 1) * NB)
        e = o + (p + 1) * NB
        R, T = diag_block([d[p * NB + 8 * i:p * NB + 8 * i + 8, rows] for i in range(NB // 8)], lane, sub)
        for i in range(NB // 8):
            rcol[o + p * NB + 8 * i:o + p * NB + 8 * i + 8, rows] = R[i]
            w_out[p * NB + 8 * i:p * NB + 8 * i + 8, e - NB:e] = T[i]
        Tm = w_out[rows, e - NB:e]
        if p + 1 < n:
            rest = slice((p + 1) * NB, w)
            rq = dot3(Tm, d[rows, rest])
            rcol[o + p * NB:o + (p + 1) * NB, rest] = rq
            rt = rq.T
            d[rest, rest] = d[rest, rest] - dot3(rt, rq)
        if e > NB:
            w_out[rows, :e - NB] = -dot3(Tm, v[rows, :e - NB])
        if p + 1 < n:
            v[rest, :e] = v[rest, :e] + dot3(rt, w_out[rows, :e])
    W = w_out[...]
    y = dot3(m_ref[:, :o + w], W, nt)
    at = 0
    for r_ref, y_ref in zip(r_refs, y_refs):
        cut = slice(at, at + r_ref.shape[1])
        r_out[:, cut] = r_ref[...]
        y_out[:, cut] = y_ref[...]
        at = cut.stop
    y_out[:, at:] = y
    x_out[...] = x_ref[...]
    x_out[:, :o + w] = x_ref[:, :o + w] + dot3(y, W)
    r_out[:, at:] = rcol[pl.ds(pl.multiple_of(idx_ref[0] * share, share), share), :]


def panel(J, n, share, grams, left, priors, moments, x, index, shares=(), ys=()):
    width = moments.shape[1]
    k = moments.shape[0]
    parts, rest = [], (J + n) * NB
    for g in grams:
        parts.append((min(g.shape[0], rest), left))
        rest -= parts[-1][0]
    wide = width if ys else n * NB
    vm = pl.BlockSpec(memory_space=pltpu.VMEM)
    shape = lambda *s: jax.ShapeDtypeStruct(s, F32)
    return pl.pallas_call(
        functools.partial(panel_kernel, J, n, share, tuple(parts), tuple(q[:2] for q in priors), len(ys)),
        out_shape=(shape(share, wide), shape(n * NB, (J + n) * NB), shape(k, wide), shape(k, width)),
        in_specs=[pl.BlockSpec(memory_space=pltpu.SMEM)] + [vm] * (len(grams) + len(priors) + 2 * len(ys) + 2),
        out_specs=(vm,) * 4,
        scratch_shapes=[
            pltpu.VMEM((width, n * NB), F32),
            pltpu.VMEM((n * NB, n * NB), F32),
            pltpu.VMEM((n * NB, (J + n) * NB), F32),
        ],
        compiler_params=pltpu.CompilerParams(vmem_limit_bytes=40 * 2**20),
        name="panels%d" % J,
    )(index, *grams, *[q[2] for q in priors], *shares, *ys, moments, x)


WIDTHS = (256, 256, 256, 256)


def exchange_orders(narrow, wide):
    first = [("narrow", 1 << b) for b in range(narrow.bit_length() - 1)]
    first += [("wide", 1 << b) for b in range(wide.bit_length() - 1)]
    second = list(first)
    if len(second) > 2:
        second[1], second[2] = second[2], second[1]
    return first, second


def swap(value, axis, bit):
    size = lax.axis_size(axis)
    return lax.ppermute(value, axis, [(i, i ^ bit) for i in range(size)])


def has_bit(axis, bit):
    return (lax.axis_index(axis) & bit) != 0


def together(*values):
    return lax.optimization_barrier(values)


def reduce_step(values, step):
    half = values.shape[0] // 2
    return values[:half] + swap(values[half:], *step)


def gather_step(values, step):
    other = swap(values, *step)
    upper = has_bit(*step)
    return jnp.concatenate([jnp.where(upper, other, values), jnp.where(upper, values, other)], axis=0)


def halves(x):
    high = lax.reduce_precision(x, 8, 7)
    return high.astype(BF), (x - high).astype(BF)


def gram_block(left, right):
    return lax.dot_general(
        left, right, (((0,), (0,)), ((), ())), precision=lax.Precision.HIGH, preferred_element_type=F32
    )


def shards(matrix, hashes, sign_bits, targets):
    width = matrix.shape[1]
    orders = exchange_orders(lax.axis_size("narrow"), lax.axis_size("wide"))
    steps = len(orders[0]) - 1
    signs = (2 * sign_bits - 1).astype(BF)
    places = lax.iota(jnp.int32, S)
    one_hots = []
    for order in orders:
        mask = jnp.int32(0)
        for step, (axis, bit) in enumerate(order[:-1]):
            mask = mask + jnp.where(has_bit(axis, bit), S >> (step + 1), 0)
        one_hots.append(jnp.where(places[:, None] == (hashes ^ mask)[None, :], signs[None, :], 0).astype(BF))

    def sketch(c, columns):
        high, low = halves(columns)
        one_hot = one_hots[c % 2]
        return jnp.dot(one_hot, high, preferred_element_type=F32) + jnp.dot(one_hot, low, preferred_element_type=F32)

    def down(c, t):
        part[c] = reduce_step(part[c], orders[c % 2][t])

    def across(c):
        part[c] = part[c] + swap(part[c], *orders[0][-1])

    def up(c, t):
        part[c] = gather_step(part[c], orders[c % 2][t])

    def line(c, lowest):
        for t in range(3, steps):
            down(c, t)
        across(c)
        for t in range(steps - 1, lowest - 1, -1):
            up(c, t)

    bounds = [sum(WIDTHS[:c]) for c in range(len(WIDTHS) + 1)]
    cols = [matrix[:, bounds[c]:bounds[c + 1]] for c in range(4)]
    part = [sketch(0, cols[0]), None, None, None]
    part[0], cols[1] = together(part[0], cols[1])
    down(0, 0)
    part[1] = sketch(1, cols[1])
    part[0], part[1], cols[2], cols[3] = together(part[0], part[1], cols[2], cols[3])
    down(1, 0)
    part[0], part[1], cols[2], cols[3] = together(part[0], part[1], cols[2], cols[3])
    down(0, 1)
    down(1, 1)
    part[2] = sketch(2, cols[2])
    part[3] = sketch(3, cols[3])
    part[0], part[1], part[2], part[3], matrix = together(*part, matrix)
    down(0, 2)
    down(1, 2)
    down(2, 0)
    down(3, 0)
    moments = jnp.dot(targets, matrix, precision=lax.Precision.HIGH, preferred_element_type=F32)
    *part, moments = together(*part, moments)
    down(2, 1)
    down(3, 1)
    line(0, 4)
    line(1, 4)
    moments = moments + swap(moments, *orders[0][0])
    *part, moments = together(*part, moments)
    down(2, 2)
    down(3, 2)
    for c in range(2):
        for t in range(min(3, steps - 1), 2, -1):
            up(c, t)
    moments = moments + swap(moments, *orders[0][1])
    *part, moments = together(*part, moments)
    up(0, 2)
    up(1, 2)
    line(2, 3)
    line(3, 3)
    moments = moments + swap(moments, *orders[0][2])
    *part, moments = together(*part, moments)
    up(0, 1)
    up(1, 1)
    for step in orders[0][3:]:
        moments = moments + swap(moments, *step)
    *part, moments = together(*part, moments)
    up(0, 0)
    up(1, 0)
    up(2, 2)
    up(3, 2)
    *part, moments = together(*part, moments)
    share = width // lax.axis_size("narrow")
    index = lax.axis_index("narrow").astype(jnp.int32).reshape(1)
    x = jnp.zeros_like(moments)
    priors, shares, ys = [], [], []

    def panels(n, grams, left, x):
        first = sum(q[1] for q in priors)
        whole = (shares, ys) if (first + n) * NB == width else ()
        r, wr, y, x = panel(first, n, share, grams, left, priors, moments, x, index, *whole)
        priors.append((first, n, wr))
        shares.append(r)
        ys.append(y)
        return x

    left = jnp.concatenate(part[:2], axis=1)
    up(2, 1)
    up(3, 1)
    column = [gram_block(left, left)]
    x = panels(2, column, 0, x)
    x = panels(1, column, 2 * NB, x)
    part[2], part[3], x = together(part[2], part[3], x)
    up(2, 0)
    up(3, 0)
    x = panels(1, column, 3 * NB, x)
    part[2], part[3], x = together(part[2], part[3], x)
    right = jnp.concatenate(part[2:], axis=1)
    column = [gram_block(left, right), gram_block(right, right)]
    x = panels(4, column, 0, x)
    return shares[-1], ys[-1], x


def solution(mesh):
    return jax.shard_map(
        shards,
        mesh=mesh,
        in_specs=(
            P(("wide", "narrow"), None),
            P(("wide", "narrow")),
            P(("wide", "narrow")),
            P(None, ("wide", "narrow")),
        ),
        out_specs=(P("narrow", None), P(), P()),
        check_vma=False,
    )
```
